256 devices in a mesh: row: 16 (over z, x_hi), col: 4 (over x_lo, core), depth: 4 (over y).
Axes of the slice: x: 4 (x_hi: 2, x_lo: 2; x = x_hi * 2 + x_lo), y: 4, z: 8, core: 2. Of those that a mesh axis runs over, the one named last changes fastest.
Arguments:
- a_tiles: bfloat16 [16, 4, 4, 4, 6, 128, 128], P('row', 'col', 'depth'), may hold values from -0.5 to 0.5
- a_index: int32 [16, 4, 4, 4, 6], P('row', 'col', 'depth'), may hold values from 0 to 127, as said below
- a_count: int32 [16, 4, 4, 4], P('row', 'col', 'depth'), may hold values from 1 to 6, as said below
- b_tiles: bfloat16 [16, 4, 4, 16, 2, 128, 128], P('row', 'col', 'depth'), may hold values from -6 to 6
- b_place: int32 [16, 4, 4, 16, 2], P('row', 'col', 'depth'), may hold values from 0 to 15, as said below
- b_count: int32 [16, 4, 4, 16], P('row', 'col', 'depth'), may hold values from 1 to 2, as said below
Outputs:
- product: float32 [64, 32, 128, 128], P(('col', 'depth'), 'row')
The draws below stay inside these ranges and needn't reach their ends.
Inputs may be any that keep to these rules, and one draw needn't show every extreme that they name: Within one panel all 6 slots name distinct places; a_index // 8 is the block row and a_index % 8 the inner block inside the panel. `a_count`: slots at or past the count carry no block; some panel is full in every draw. Within one panel all 2 slots name distinct places; b_place // 2 is the inner block and b_place % 2 the block column inside the panel. `b_count`: slots at or past the count carry no block; some panel is full in every draw.
All inputs are finite; a program needn't handle non-finite values.
Results may differ from the reference program's by a relative error of at most 0.0003.
Values may be sent and summed in bfloat16 or wider, within the bound.
No kernel may reach another device: no remote copies, remote signals or barrier semaphores. Data moves between devices by JAX's collectives and lax.ppermute only.
A program may use at most 192 MiB of HBM per device.

```python
import jax
import jax.numpy as jnp
from jax import lax

TILE = 128
BK = 8
NCB = 2
SA = 6
SB = 2
MBR = 16
N_ROW = 16
N_COL = 4
N_DEPTH = 4


def distinct_places(key, panels, places, taken):
    scores = jax.random.randint(key, (panels, places), 0, 2 ** 16, dtype=jnp.int32)
    scores = scores * places + jnp.arange(places, dtype=jnp.int32)[None, :]
    order = jnp.argsort(scores, axis=1, stable=True)[:, :taken]
    return order.astype(jnp.int32)


def hot_inner(key):
    return jax.random.randint(jax.random.fold_in(key, 77), (N_ROW, N_COL, N_DEPTH), 0, BK, dtype=jnp.int32)


def drifted(key, hot):
    first_key, second_key = jax.random.split(key, 2)
    moved = jax.random.randint(first_key, hot.shape, 0, 4, dtype=jnp.int32) == 0
    offset = jax.random.randint(second_key, hot.shape, 1, BK, dtype=jnp.int32)
    return jnp.where(moved, (hot + offset) % BK, hot)


def forced_order(order, limit, taken):
    flat = jnp.arange(order.shape[0], dtype=jnp.int32)[:, None]
    span = jnp.arange(taken, dtype=jnp.int32)[None, :]
    return jnp.where(flat == 0, limit - 1 - span, jnp.where(flat == 1, span, order))


def draw_a_index(key, part):
    panels = N_ROW * N_COL * N_DEPTH * N_COL
    rows = distinct_places(jax.random.fold_in(key, 101), panels, MBR, SA)
    rows = forced_order(rows, MBR, SA)
    hot = jnp.transpose(hot_inner(key), (0, 2, 1))[:, None, :, :, None]
    hot = jnp.broadcast_to(hot, (N_ROW, N_COL, N_DEPTH, N_COL, SA))
    inner = drifted(jax.random.fold_in(key, 111), hot).reshape(panels, SA)
    inner = inner.at[0, 0].set(BK - 1).at[1, 0].set(0)
    places = rows * BK + inner
    return places.reshape(N_ROW, N_COL, N_DEPTH, N_COL, SA).astype(jnp.int32)


def draw_a_count(key, part):
    base_key = jax.random.fold_in(key, 202)
    first_key, second_key, third_key, fourth_key = jax.random.split(base_key, 4)
    weight = 1 + jax.random.randint(first_key, (1, N_COL, N_DEPTH, 1), 0, 6, dtype=jnp.int32) * jax.random.randint(second_key, (1, N_COL, N_DEPTH, 1), 0, 6, dtype=jnp.int32) // 5
    raw_draw = jax.random.randint(third_key, (N_ROW, N_COL, N_DEPTH, N_COL), 0, SA, dtype=jnp.int32)
    counts = jnp.minimum(1 + raw_draw * weight // 6, SA).reshape(-1)
    chosen = jax.random.randint(fourth_key, (), 0, counts.shape[0], dtype=jnp.int32)
    counts = counts.at[chosen].set(SA)
    return counts.reshape(N_ROW, N_COL, N_DEPTH, N_COL).astype(jnp.int32)


def draw_b_place(key, part):
    panels = N_ROW * N_COL * N_DEPTH * N_ROW
    columns = distinct_places(jax.random.fold_in(key, 303), panels, NCB, SB)
    columns = forced_order(columns, NCB, SB)
    hot = jnp.transpose(hot_inner(key), (1, 2, 0))[None, :, :, :, None]
    hot = jnp.broadcast_to(hot, (N_ROW, N_COL, N_DEPTH, N_ROW, SB))
    inner = drifted(jax.random.fold_in(key, 313), hot).reshape(panels, SB)
    inner = inner.at[0, 0].set(BK - 1).at[1, 0].set(0)
    places = inner * NCB + columns
    return places.reshape(N_ROW, N_COL, N_DEPTH, N_ROW, SB).astype(jnp.int32)


def draw_b_count(key, part):
    base_key = jax.random.fold_in(key, 404)
    first_key, second_key = jax.random.split(base_key, 2)
    counts = jax.random.randint(first_key, (N_ROW * N_COL * N_DEPTH * N_ROW,), 1, SB + 1, dtype=jnp.int32)
    chosen = jax.random.randint(second_key, (), 0, counts.shape[0], dtype=jnp.int32)
    counts = counts.at[chosen].set(SB)
    return counts.reshape(N_ROW, N_COL, N_DEPTH, N_ROW).astype(jnp.int32)


def steps_of(own_key, dims, cuts, smallest, largest):
    loudness = 1.0
    for dim, blocks in cuts:
        heights = jax.random.uniform(jax.random.fold_in(jax.random.fold_in(own_key, 6), dim), (blocks,), jnp.float32, smallest / len(cuts), largest / len(cuts))
        loudness = loudness * jnp.repeat(jnp.exp(heights), dims[dim] // blocks).reshape((-1,) + (1,) * (len(dims) - 1 - dim))
    return loudness


def bell_draw(stream_key, shape, deviation, bound, cuts=(), kind=jnp.bfloat16):
    values = jax.random.normal(stream_key, shape, jnp.float32) * deviation
    if len(cuts) > 0:
        values = steps_of(stream_key, shape, cuts, -0.22, 0.18) * values
    return jnp.clip(values, min=-bound, max=bound).astype(kind)


def setup_inputs(seed: int = 0) -> dict:
    key_of = jax.random.split(jax.random.key(seed), 7)
    a_tiles = bell_draw(key_of[0], (N_ROW, N_COL, N_DEPTH, N_COL, SA, TILE, TILE), TILE ** -0.5, 0.5, ((0, 16), (1, 4), (2, 4)))
    a_index = draw_a_index(jax.random.fold_in(key_of[6], 71), 0)
    a_count = draw_a_count(jax.random.fold_in(key_of[6], 71), 0)
    b_tiles = bell_draw(key_of[3], (N_ROW, N_COL, N_DEPTH, N_ROW, SB, TILE, TILE), 1.0, 6.0, ((0, 16), (1, 4), (2, 4)))
    b_place = draw_b_place(jax.random.fold_in(key_of[6], 71), 0)
    b_count = draw_b_count(jax.random.fold_in(key_of[6], 71), 0)
    return {"a_tiles": a_tiles, "a_index": a_index, "a_count": a_count, "b_tiles": b_tiles, "b_place": b_place, "b_count": b_count}


def reference(a_tiles, a_index, a_count, b_tiles, b_place, b_count):
    slot_range = jnp.arange(SA, dtype=jnp.int32)
    right_range = jnp.arange(SB, dtype=jnp.int32)
    column_range = jnp.arange(NCB, dtype=jnp.int32)

    def one_pair(pair_index):
        col_pos = pair_index // N_ROW
        row_pos = pair_index % N_ROW

        def one_group(total, group_pos):
            left_tiles = a_tiles[group_pos, col_pos]
            left_index = a_index[group_pos, col_pos]
            left_count = a_count[group_pos, col_pos]
            right_tiles = jnp.transpose(b_tiles[row_pos, :, :, group_pos], (1, 0, 2, 3, 4))
            right_place = jnp.transpose(b_place[row_pos, :, :, group_pos], (1, 0, 2))
            right_count = jnp.transpose(b_count[row_pos, :, :, group_pos], (1, 0))
            left_live = slot_range < left_count[..., None]
            right_live = right_range < right_count[..., None]
            block_row = left_index // BK
            block_inner = left_index % BK
            matched = (right_place[..., None, :] // NCB == block_inner[..., :, None]) & left_live[..., :, None] & right_live[..., None, :]
            spread = matched[..., None] & ((right_place % NCB)[..., None, :, None] == column_range)
            picked = jnp.einsum("lbtsc,lbsjk->lbtcjk", spread.astype(jnp.float32), right_tiles.astype(jnp.float32), precision=lax.Precision.HIGHEST)
            product = jnp.einsum("lbtij,lbtcjk->lbtcik", left_tiles.astype(jnp.float32), picked, precision=lax.Precision.HIGHEST)
            target = (block_row[..., None] * NCB + column_range).reshape(-1).astype(jnp.int32)
            total = total.at[target].add(product.reshape(-1, TILE, TILE))
            return total, None

        start = jnp.zeros((MBR * NCB, TILE, TILE), jnp.float32)
        result, _ = lax.scan(one_group, start, jnp.arange(N_ROW, dtype=jnp.int32))
        return result

    outputs = lax.map(one_pair, jnp.arange(N_COL * N_ROW, dtype=jnp.int32))
    outputs = outputs.reshape(N_COL, N_ROW, MBR, NCB, TILE, TILE)
    outputs = jnp.transpose(outputs, (0, 2, 1, 3, 4, 5))
    return outputs.reshape(N_COL * MBR, N_ROW * NCB, TILE, TILE)
```

```python
import functools

import jax
import jax.numpy as jnp
from jax import lax
from jax.experimental import pallas as pl
from jax.experimental.pallas import tpu as pltpu
from jax.sharding import PartitionSpec as P

NZ = 8
SA = 6
SB = 2
PANELS = 4
ATILES = PANELS * SA
TILE = 128
LEFT_ROWS = ATILES * TILE
LEFT_SIDE = 16
RIGHT_ROWS = 8 * SB * TILE
RIGHT_SIDE = 32
RIGHT_PART = RIGHT_ROWS + RIGHT_SIDE
QUARTER = 1024
BOTH = ("row", "col")
ALL = ("row", "col", "depth")
HBM = pl.BlockSpec(memory_space=pltpu.HBM)
VMEM = pl.BlockSpec(memory_space=pltpu.VMEM)
SMEM = pl.BlockSpec(memory_space=pltpu.SMEM)


def gid(z, h, l, c):
    return ((z * 2 + h) * 2 + l) * 2 + c


def group():
    return [(z, h, l, c) for z in range(NZ) for h in range(2) for l in range(2) for c in range(2)]


def swap_route():
    return [(gid(z, h, l, c), gid(z, c, 1 - l, h)) for z, h, l, c in group()]


def home_route(d):
    return [(s * 4 + y, t * 4 + (y + d) % 4) for s, t in swap_route() for y in range(4)]


def z_route(d):
    return [(2 * z + h, 2 * ((z + d) % NZ) + h) for z in range(NZ) for h in range(2)]


def y_route(d):
    return [(y, (y + d) % 4) for y in range(4)]


def outer_route():
    return [(gid(z, h, l, c), gid(z, 1 - h, 1 - l, c)) for z, h, l, c in group()]


CORE_ROUTE = [(i, i ^ 1) for i in range(4)]
INNER_ROUTE = [(i, i ^ 2) for i in range(4)]


def copy_all(pairs, sem):
    copies = []
    for src, dst in pairs:
        copy = pltpu.make_async_copy(src, dst, sem.at[len(copies)])
        copy.start()
        copies.append(copy)
    return copies


def pack_kernel(ids, index, sizes, place, right_sizes, tiles, right_tiles, left, mine, theirs, wide, sem):
    c = ids[3]
    pairs = [(tiles, left.at[pl.ds(0, LEFT_ROWS)])]
    for z in range(NZ):
        rows = pl.ds(z * 256, 256)
        pairs.append((right_tiles.at[z * 2 + c], mine.at[rows]))
        pairs.append((right_tiles.at[z * 2 + 1 - c], theirs.at[rows]))
    copies = copy_all(pairs, sem)
    wide[...] = jnp.zeros_like(wide)
    wide[0:PANELS, 0:SA] = index[...].astype(jnp.float32)
    wide[8:9, 0:PANELS] = sizes[...].astype(jnp.float32)
    wide[16:32, 0:SB] = place[...].astype(jnp.float32)
    wide[32:33, 0:16] = right_sizes[...].astype(jnp.float32)
    left[LEFT_ROWS:, :] = wide[0:16, :].astype(jnp.bfloat16)
    for out in (mine, theirs):
        out[RIGHT_ROWS:, :] = wide[16:48, :].astype(jnp.bfloat16)
    for copy in copies:
        copy.wait()


def pack(ids, index, sizes, place, right_sizes, tiles, right_tiles):
    return pl.pallas_call(
        pack_kernel,
        out_shape=[jax.ShapeDtypeStruct((LEFT_ROWS + LEFT_SIDE, TILE), jnp.bfloat16)]
        + [jax.ShapeDtypeStruct((RIGHT_PART, TILE), jnp.bfloat16)] * 2,
        in_specs=[SMEM, VMEM, VMEM, VMEM, VMEM, HBM, HBM],
        out_specs=[VMEM] * 3,
        scratch_shapes=[pltpu.VMEM((48, TILE), jnp.float32), pltpu.SemaphoreType.DMA((17,))],
        name="pack",
    )(ids, index, sizes, place, right_sizes, tiles, right_tiles)


def kernel(deltas, nparts, first, outs_rows, nafter, *refs):
    n = len(deltas)
    refs = list(refs)

    def take(k):
        got = refs[:k]
        del refs[:k]
        return got

    (ids,) = take(1)
    lefts = take(n * nparts)
    rights = take(4)
    c_in = None if first else take(1)[0]
    take(nafter)
    outs = take(len(outs_rows))
    abuf, bbuf, acc, side, side_int, meta, work, side_sem, in_sem, meta_sem = refs

    z, h, l, c, y = (ids[k] for k in range(5))
    right_at = n * LEFT_SIDE
    pairs = []
    for s in range(n):
        part = lefts[s * nparts + nparts - 1]
        pairs.append(
            (part.at[pl.ds(part.shape[0] - LEFT_SIDE, LEFT_SIDE)], side.at[pl.ds(s * LEFT_SIDE, LEFT_SIDE)])
        )
    for k in range(4):
        for rel in range(2):
            pairs.append(
                (
                    rights[k].at[pl.ds(rel * RIGHT_PART + RIGHT_ROWS, RIGHT_SIDE)],
                    side.at[pl.ds(right_at + (k * 2 + rel) * RIGHT_SIDE, RIGHT_SIDE)],
                )
            )
    side_copies = copy_all(pairs, side_sem)
    size = LEFT_ROWS // nparts
    pairs = []
    for p in range(n * nparts):
        pairs.append((lefts[p].at[pl.ds(0, size)], abuf.at[pl.ds(p * size, size)]))
    for s, delta in enumerate(deltas):
        zs = (z + delta) & (NZ - 1)
        for k in range(4):
            for rel in range(2):
                rows = pl.ds(pl.multiple_of(rel * RIGHT_PART + zs * 256, 16), 256)
                pairs.append((rights[k].at[rows], bbuf.at[pl.ds((s * 8 + k * 2 + rel) * 256, 256)]))
    copies = copy_all(pairs, in_sem)

    for copy in side_copies:
        copy.wait()
    side_int[...] = side[...].astype(jnp.float32).astype(jnp.int32)
    copy = pltpu.make_async_copy(side_int, meta, meta_sem)
    copy.start()
    if first:
        acc[...] = jnp.zeros_like(acc)
    else:
        acc[pl.ds(0, 64 * TILE)] = c_in[...]
    copy.wait()

    count = jnp.int32(0)
    for s, delta in enumerate(deltas):
        a = ((z + delta) & (NZ - 1)) * 2 + c
        ra = s * LEFT_SIDE

        def panel(k, count, s=s, a=a, ra=ra):
            block_at = k >> 1
            b = (l ^ ((block_at ^ (block_at >> 1)) & 1)) * 2 + (c ^ (k & 1))
            half = (h ^ (block_at >> 1) ^ c) * 32
            rb = right_at + k * RIGHT_SIDE
            live_a = meta[ra + 8, b]
            live_b = meta[rb + 16, a]
            ta = s * ATILES + b * SA
            tb = s * 16 + k * 2
            for q in range(SB):
                place = meta[rb + a, q]
                for t in range(SA):
                    index = meta[ra + b, t]
                    i = index >> 3
                    chunk = ((i >> 2) - y) & 3
                    spot = chunk ^ (chunk >> 1)
                    block = half + (spot * 4 + (i & 3)) * 2 + (place & 1)
                    hit = ((index & 7) == (place >> 1)) & (t < live_a) & (q < live_b)
                    work[count] = (block << 20) | ((tb + q) << 10) | (ta + t)
                    count = count + hit.astype(jnp.int32)
            return count

        count = lax.fori_loop(0, 8, panel, count)
    for k in range(3):
        work[count + k] = jnp.int32(64 << 20)

    for copy in copies:
        copy.wait()

    def rows_of(k):
        return pl.ds(pl.multiple_of(k * TILE, TILE), TILE)

    def products(g, carry):
        for k in range(4):
            w = work[g * 4 + k]
            block = rows_of(w >> 20)
            acc[block] = acc[block] + jnp.dot(
                abuf[rows_of(w & 1023)], bbuf[rows_of((w >> 10) & 1023)], preferred_element_type=jnp.float32
            )
        return carry

    lax.fori_loop(0, (count + 3) >> 2, products, 0)

    for (start, size), out in zip(outs_rows, outs):
        out[...] = acc[pl.ds(start * TILE, size * TILE)]


def multiply(deltas, ids, lefts, rights, total, outs_rows, after):
    n = len(deltas)
    nparts = len(lefts) // n
    first = total is None
    operands = [ids, *lefts, *rights] + ([] if first else [total]) + list(after)
    sides = n * LEFT_SIDE + 8 * RIGHT_SIDE
    return pl.pallas_call(
        functools.partial(kernel, deltas, nparts, first, outs_rows, len(after)),
        out_shape=[jax.ShapeDtypeStruct((k * TILE, TILE), jnp.float32) for _, k in outs_rows],
        in_specs=[SMEM] + [HBM] * (len(lefts) + 4) + ([] if first else [VMEM]) + [HBM] * len(after),
        out_specs=[VMEM] * len(outs_rows),
        scratch_shapes=[
            pltpu.VMEM((n * LEFT_ROWS, TILE), jnp.bfloat16),
            pltpu.VMEM((n * 16 * TILE, TILE), jnp.bfloat16),
            pltpu.VMEM((65 * TILE, TILE), jnp.float32),
            pltpu.VMEM((sides, TILE), jnp.bfloat16),
            pltpu.VMEM((sides, TILE), jnp.int32),
            pltpu.SMEM((sides, TILE), jnp.int32),
            pltpu.SMEM((n * 96 + 8,), jnp.int32),
            pltpu.SemaphoreType.DMA((n + 8,)),
            pltpu.SemaphoreType.DMA((n * nparts + 8 * n,)),
            pltpu.SemaphoreType.DMA,
        ],
        compiler_params=pltpu.CompilerParams(vmem_limit_bytes=(24 + 2 * n) * 1024 * 1024),
        cost_estimate=pl.CostEstimate(
            flops=n * 40_000_000, bytes_accessed=8_000_000 + n * 4_000_000, transcendentals=0
        ),
        name="products_%s" % "_".join(str(d & 7) for d in deltas),
    )(*operands)


def shards(a_tiles, a_index, a_count, b_tiles, b_place, b_count):
    row = lax.axis_index("row")
    col = lax.axis_index("col")
    y = lax.axis_index("depth")
    ids = jnp.stack([row >> 1, row & 1, col >> 1, col & 1, y, y, y, y]).astype(jnp.int32)
    send = lax.ppermute
    barrier = lax.optimization_barrier

    left, mine, theirs = pack(
        ids,
        a_index.reshape(PANELS, SA),
        a_count.reshape(1, PANELS),
        b_place.reshape(16, SB),
        b_count.reshape(1, 16),
        a_tiles.reshape(LEFT_ROWS, TILE),
        b_tiles.reshape(16, SB * TILE, TILE),
    )
    own = send(left, BOTH, swap_route())
    right = jnp.concatenate([mine, send(theirs, "col", CORE_ROUTE)], axis=0)
    own, right = barrier((own, right))

    def onward(f, b):
        return send(f, "row", z_route(1)), send(b, "row", z_route(-1))

    def inner(x):
        return send(x, "col", INNER_ROUTE)

    def outer(x):
        return send(x, BOTH, outer_route())

    f1, b1 = onward(own, own)
    rest = 2 * RIGHT_PART - QUARTER
    in1, out1 = inner(right[QUARTER:]), outer(right[:rest])
    f1, b1, in1, out1 = barrier((f1, b1, in1, out1))

    f2, b2 = onward(f1, b1)
    in2 = inner(jnp.concatenate([right[:QUARTER], out1[:RIGHT_PART]], axis=0))
    out2 = outer(jnp.concatenate([right[rest:], in1[RIGHT_PART - QUARTER :]], axis=0))
    f2, b2, in2, out2 = barrier((f2, b2, in2, out2))

    f3, b3 = onward(f2, b2)
    rights = [
        right,
        jnp.concatenate([in2[:QUARTER], in1], axis=0),
        jnp.concatenate([out1, out2[:QUARTER]], axis=0),
        jnp.concatenate([in2[QUARTER:], out2[QUARTER:]], axis=0),
    ]
    whole = ((0, 64),)
    (total,) = multiply((0, -1, 1, -2, 2), ids, [own, f1, b1, f2, b2], rights, None, whole, [])

    f3, b3, total = barrier((f3, b3, total))
    half = LEFT_ROWS // 2
    far = [send(f3[:half], "row", z_route(1)), send(b3[half:], "row", z_route(-1))]
    (total,) = multiply((-3, 3), ids, [f3, b3], rights, total, whole, [])
    kept, other = multiply((4,), ids, far, rights, total, ((0, 32), (32, 32)), [])

    other = send(other, "col", CORE_ROUTE)
    half = 4 * TILE

    def unit(k, kept=kept, other=other):
        return kept[k * half : (k + 1) * half] + other[k * half : (k + 1) * half]

    units = barrier((unit(6), unit(7), unit(3), unit(4)))
    up2 = send(units[0], "depth", y_route(1))
    down2 = send(units[1], "depth", y_route(-1))
    up1 = send(units[2], "depth", y_route(1))
    down1 = send(units[3], "depth", y_route(-1))
    up3, down3, kept, other = barrier((unit(2) + up2, unit(5) + down2, kept, other))
    up3 = send(up3, ALL, home_route(1))
    down3 = send(down3, ALL, home_route(-1))
    low = send(unit(0, kept, other) + down1, BOTH, swap_route()) + up3
    high = send(unit(1, kept, other) + up1, BOTH, swap_route()) + down3
    return jnp.concatenate([low, high], axis=0).reshape(4, 2, TILE, TILE)


def solution(mesh):
    placed = (
        P("row", "col", "depth", None, None, None, None),
        P("row", "col", "depth", None, None),
        P("row", "col", "depth", None),
        P("row", "col", "depth", None, None, None, None),
        P("row", "col", "depth", None, None),
        P("row", "col", "depth", None),
    )
    return jax.shard_map(
        shards,
        mesh=mesh,
        in_specs=placed,
        out_specs=P(("col", "depth"), "row", None, None),
        check_vma=False,
    )
```

```python
import functools

import jax
import jax.numpy as jnp
from jax import lax
from jax.experimental import pallas as pl
from jax.experimental.pallas import tpu as pltpu
from jax.sharding import PartitionSpec as P

NZ = 8
SA = 6
SB = 2
PANELS = 4
ATILES = PANELS * SA
TILE = 128
LEFT_ROWS = ATILES * TILE
RIGHT_ROWS = 8 * SB * TILE
QUARTER = 1024
BOTH = ("row", "col")
ALL = ("row", "col", "depth")
HBM = pl.BlockSpec(memory_space=pltpu.HBM)
VMEM = pl.BlockSpec(memory_space=pltpu.VMEM)
SMEM = pl.BlockSpec(memory_space=pltpu.SMEM)


def gid(z, h, l, c):
    return ((z * 2 + h) * 2 + l) * 2 + c


def group():
    return [(z, h, l, c) for z in range(NZ) for h in range(2) for l in range(2) for c in range(2)]


def swap_route():
    return [(gid(z, h, l, c), gid(z, c, 1 - l, h)) for z, h, l, c in group()]


def home_route(d):
    return [(s * 4 + y, t * 4 + (y + d) % 4) for s, t in swap_route() for y in range(4)]


def z_route(d):
    return [(2 * z + h, 2 * ((z + d) % NZ) + h) for z in range(NZ) for h in range(2)]


def y_route(d):
    return [(y, (y + d) % 4) for y in range(4)]


def outer_route():
    return [(gid(z, h, l, c), gid(z, 1 - h, 1 - l, c)) for z, h, l, c in group()]


BITS = (3, 4, 5, 1, 0, 2)


def slot(offset):
    return sum(((offset >> bit) & 1) << k for k, bit in enumerate(BITS))


CORE_ROUTE = [(i, i ^ 1) for i in range(4)]
INNER_ROUTE = [(i, i ^ 2) for i in range(4)]


def copy_all(pairs, sem):
    copies = []
    for src, dst in pairs:
        copy = pltpu.make_async_copy(src, dst, sem.at[len(copies)])
        copy.start()
        copies.append(copy)
    return copies


def kernel(deltas, parts, tiles, first, outs_rows, *refs):
    n = len(deltas)
    nparts = len(parts)
    refs = list(refs)

    def take(k):
        got = refs[:k]
        del refs[:k]
        return got

    ids, meta = take(2)
    lefts = take(n * nparts)
    rights = take(4)
    c_in = None if first else take(1)[0]
    outs = take(len(outs_rows))
    abuf, bbuf, acc, work, in_sem = refs

    z, h, l, c, y = (ids[k] for k in range(5))
    me = gid(z, h, l, c)
    pairs = []
    for s in range(n):
        spot = s * tiles * TILE
        for p, (start, size) in enumerate(parts):
            pairs.append((lefts[s * nparts + p].at[pl.ds(start, size)], abuf.at[pl.ds(spot, size)]))
            spot += size
    for s, delta in enumerate(deltas):
        zs = (z + delta) & (NZ - 1)
        for k in range(4):
            for rel in range(2):
                rows = pl.ds(pl.multiple_of(rel * RIGHT_ROWS + zs * 256, 256), 256)
                pairs.append((rights[k].at[rows], bbuf.at[pl.ds((s * 8 + k * 2 + rel) * 256, 256)]))
    copies = copy_all(pairs, in_sem)

    if first:
        acc[...] = jnp.zeros_like(acc)
    else:
        acc[pl.ds(0, 64 * TILE)] = c_in[...]

    count = jnp.int32(0)
    for s, delta in enumerate(deltas):
        zs = (z + delta) & (NZ - 1)
        ra = slot(gid(zs, c, 1 - l, h) ^ me)

        def panel(k, count, s=s, zs=zs, ra=ra):
            at = k >> 1
            b_l = l ^ ((at ^ (at >> 1)) & 1)
            b_c = c ^ (k & 1)
            b = b_l * 2 + b_c
            rb = slot(gid(z, h ^ (at >> 1), b_l, b_c) ^ me)
            half = (h ^ (at >> 1) ^ c) * 32
            base = 32 + (zs * 2 + c) * 4
            live_a = meta[ra, b * 8 + 6]
            live_b = meta[rb, base + 2]
            ta = s * tiles + b * SA
            tb = s * 16 + k * 2
            for q in range(SB):
                place = meta[rb, base + q]
                for t in range(SA):
                    index = meta[ra, b * 8 + t]
                    i = index >> 3
                    chunk = ((i >> 2) - y) & 3
                    spot = chunk ^ (chunk >> 1)
                    block = half + (spot * 4 + (i & 3)) * 2 + (place & 1)
                    hit = ((index & 7) == (place >> 1)) & (t < live_a) & (q < live_b)
                    work[count] = (block << 20) | ((tb + q) << 10) | (ta + t)
                    count = count + hit.astype(jnp.int32)
            return count

        count = lax.fori_loop(0, 8, panel, count)
    for k in range(3):
        work[count + k] = jnp.int32(64 << 20)

    for copy in copies:
        copy.wait()

    def rows_of(k):
        return pl.ds(pl.multiple_of(k * TILE, TILE), TILE)

    def products(g, carry):
        for k in range(4):
            w = work[g * 4 + k]
            block = rows_of(w >> 20)
            acc[block] = acc[block] + jnp.dot(
                abuf[rows_of(w & 1023)], bbuf[rows_of((w >> 10) & 1023)], preferred_element_type=jnp.float32
            )
        return carry

    lax.fori_loop(0, (count + 3) >> 2, products, 0)

    for (start, size), out in zip(outs_rows, outs):
        out[...] = acc[pl.ds(start * TILE, size * TILE)]


def multiply(deltas, parts, tiles, ids, meta, lefts, rights, total, outs_rows):
    n = len(deltas)
    first = total is None
    operands = [ids, meta, *lefts, *rights] + ([] if first else [total])
    return pl.pallas_call(
        functools.partial(kernel, deltas, parts, tiles, first, outs_rows),
        out_shape=[jax.ShapeDtypeStruct((k * TILE, TILE), jnp.float32) for _, k in outs_rows],
        in_specs=[SMEM, SMEM] + [HBM] * (len(lefts) + 4) + ([] if first else [VMEM]),
        out_specs=[VMEM] * len(outs_rows),
        scratch_shapes=[
            pltpu.VMEM((n * tiles * TILE, TILE), jnp.bfloat16),
            pltpu.VMEM((n * 16 * TILE, TILE), jnp.bfloat16),
            pltpu.VMEM((65 * TILE, TILE), jnp.float32),
            pltpu.SMEM((n * 96 + 8,), jnp.int32),
            pltpu.SemaphoreType.DMA((len(lefts) + 8 * n,)),
        ],
        compiler_params=pltpu.CompilerParams(vmem_limit_bytes=(24 + 2 * n) * 1024 * 1024),
        cost_estimate=pl.CostEstimate(
            flops=n * 40_000_000, bytes_accessed=8_000_000 + n * 4_000_000, transcendentals=0
        ),
        name="products_%s" % "_".join(str(d & 7) for d in deltas),
    )(*operands)


send = lax.ppermute
barrier = lax.optimization_barrier


def onward(f, b):
    return send(f, "row", z_route(1)), send(b, "row", z_route(-1))


def inner(x):
    return send(x, "col", INNER_ROUTE)


def outer(x):
    return send(x, BOTH, outer_route())


REST = 2 * RIGHT_ROWS - QUARTER


def spread(meta, bit):
    return jnp.concatenate([meta, send(meta, BOTH, [(i, i ^ (1 << bit)) for i in range(64)])], axis=0)


def shards(a_tiles, a_index, a_count, b_tiles, b_place, b_count):
    row = lax.axis_index("row")
    col = lax.axis_index("col")
    y = lax.axis_index("depth")
    core = col & 1
    ids = jnp.stack([row >> 1, row & 1, col >> 1, core, y, y, y, y]).astype(jnp.int32)

    own = send(a_tiles.reshape(LEFT_ROWS, TILE), BOTH, swap_route())
    tiles = b_tiles.reshape(NZ, 2, SB * TILE, TILE)
    mine = lax.dynamic_index_in_dim(tiles, core, 1, keepdims=False).reshape(RIGHT_ROWS, TILE)
    theirs = lax.dynamic_index_in_dim(tiles, 1 - core, 1, keepdims=False).reshape(RIGHT_ROWS, TILE)
    right = jnp.concatenate([mine, send(theirs, "col", CORE_ROUTE)], axis=0)
    left_meta = jnp.pad(a_index.reshape(PANELS, SA), ((0, 0), (0, 2))) + jnp.pad(
        a_count.reshape(PANELS, 1), ((0, 0), (6, 1))
    )
    right_meta = jnp.pad(b_place.reshape(16, SB), ((0, 0), (0, 2))) + jnp.pad(
        b_count.reshape(16, 1), ((0, 0), (2, 1))
    )
    meta = jnp.concatenate(
        [left_meta.reshape(1, 32), right_meta.reshape(1, 64), jnp.zeros((1, 32), jnp.int32)], axis=1
    )
    for bit in BITS[:3]:
        meta = spread(meta, bit)
    own, meta = barrier((own, meta))

    f1, b1 = onward(own, own)
    meta = spread(meta, BITS[3])
    right, meta = barrier((right, meta))
    in1, out1 = inner(right[QUARTER:]), outer(right[:REST])
    meta = spread(meta, BITS[4])
    f1, b1 = barrier((f1, b1))

    f2, b2 = onward(f1, b1)
    in1, out1, meta = barrier((in1, out1, meta))
    meta = spread(meta, BITS[5])
    in2 = jnp.concatenate([right[:QUARTER], out1[:RIGHT_ROWS]], axis=0)
    out2 = jnp.concatenate([right[REST:], in1[RIGHT_ROWS - QUARTER :]], axis=0)
    in2, out2, meta = barrier((in2, out2, meta))
    in2, out2 = inner(in2), outer(out2)
    f2, b2 = barrier((f2, b2))

    f3, b3 = onward(f2, b2)
    rights = [
        right,
        jnp.concatenate([in2[:QUARTER], in1], axis=0),
        jnp.concatenate([out1, out2[:QUARTER]], axis=0),
        jnp.concatenate([in2[QUARTER:], out2[QUARTER:]], axis=0),
    ]
    near = LEFT_ROWS // 2
    one = ((0, LEFT_ROWS),)
    two = ((0, near), (0, LEFT_ROWS - near))
    whole = ((0, 64),)
    (total,) = multiply(
        (0, -1, 1, -2, 2), one, ATILES, ids, meta, [own, f1, b1, f2, b2], rights, None, whole
    )
    f3, b3, total = barrier((f3, b3, total))
    far = [send(f3[:near], "row", z_route(1)), send(b3[near:], "row", z_route(-1))]
    (total,) = multiply((-3, 3), one, ATILES, ids, meta, [f3, b3], rights, total, whole)
    kept, other = multiply((4,), two, ATILES, ids, meta, far, rights, total, ((0, 32), (32, 32)))

    other = send(other, "col", CORE_ROUTE)
    half = 4 * TILE

    def unit(k, count=1):
        rows = slice(k * half, (k + count) * half)
        return kept[rows] + other[rows]

    units = barrier((unit(6), unit(7), unit(3), unit(4), unit(0, 2)))
    up2 = send(units[0], "depth", y_route(1))
    down2 = send(units[1], "depth", y_route(-1))
    still = send(units[4], BOTH, swap_route())
    up1 = send(units[2], ALL, home_route(1))
    down1 = send(units[3], ALL, home_route(-1))
    up2, down2, still = barrier((up2, down2, still))
    up3 = send(unit(2) + up2, ALL, home_route(1))
    down3 = send(unit(5) + down2, ALL, home_route(-1))
    low = still[:half] + down1 + up3
    high = still[half:] + up1 + down3
    return jnp.concatenate([low, high], axis=0).reshape(4, 2, TILE, TILE)


def solution(mesh):
    placed = (
        P("row", "col", "depth", None, None, None, None),
        P("row", "col", "depth", None, None),
        P("row", "col", "depth", None),
        P("row", "col", "depth", None, None, None, None),
        P("row", "col", "depth", None, None),
        P("row", "col", "depth", None),
    )
    return jax.shard_map(
        shards,
        mesh=mesh,
        in_specs=placed,
        out_specs=P(("col", "depth"), "row", None, None),
        check_vma=False,
    )
```

```python
import functools

import jax
import jax.numpy as jnp
from jax import lax
from jax.experimental import pallas as pl
from jax.experimental.pallas import tpu as pltpu
from jax.sharding import PartitionSpec as P

NZ = 8
SA = 6
SB = 2
PANELS = 4
ATILES = PANELS * SA
TILE = 128
LEFT_ROWS = ATILES * TILE
RIGHT_ROWS = 8 * SB * TILE
QUARTER = 1024
BOTH = ("row", "col")
ALL = ("row", "col", "depth")
HBM = pl.BlockSpec(memory_space=pltpu.HBM)
VMEM = pl.BlockSpec(memory_space=pltpu.VMEM)
SMEM = pl.BlockSpec(memory_space=pltpu.SMEM)


def gid(z, h, l, c):
    return ((z * 2 + h) * 2 + l) * 2 + c


def group():
    return [(z, h, l, c) for z in range(NZ) for h in range(2) for l in range(2) for c in range(2)]


def swap_route():
    return [(gid(z, h, l, c), gid(z, c, 1 - l, h)) for z, h, l, c in group()]


def home_route(d):
    return [(s * 4 + y, t * 4 + (y + d) % 4) for s, t in swap_route() for y in range(4)]


def z_route(d):
    return [(2 * z + h, 2 * ((z + d) % NZ) + h) for z in range(NZ) for h in range(2)]


def y_route(d):
    return [(y, (y + d) % 4) for y in range(4)]


def outer_route():
    return [(gid(z, h, l, c), gid(z, 1 - h, 1 - l, c)) for z, h, l, c in group()]


BITS = (3, 4, 1, 0, 2, 5)


def slot(offset):
    return sum(((offset >> bit) & 1) << k for k, bit in enumerate(BITS))


CORE_ROUTE = [(i, i ^ 1) for i in range(4)]
INNER_ROUTE = [(i, i ^ 2) for i in range(4)]


def copy_all(pairs, sem):
    copies = []
    for src, dst in pairs:
        copy = pltpu.make_async_copy(src, dst, sem.at[len(copies)])
        copy.start()
        copies.append(copy)
    return copies


def kernel(deltas, parts, tiles, first, outs_rows, *refs):
    n = len(deltas)
    nparts = len(parts)
    refs = list(refs)

    def take(k):
        got = refs[:k]
        del refs[:k]
        return got

    ids, meta = take(2)
    lefts = take(n * nparts)
    right, in1, in2, out1, out2 = take(5)
    c_in = None if first else take(1)[0]
    outs = take(len(outs_rows))
    abuf, bbuf, acc, work, in_sem = refs

    z, h, l, c, y = (ids[k] for k in range(5))
    me = gid(z, h, l, c)
    pairs = []
    for s in range(n):
        spot = s * tiles * TILE
        for p, (start, size) in enumerate(parts):
            pairs.append((lefts[s * nparts + p].at[pl.ds(start, size)], abuf.at[pl.ds(spot, size)]))
            spot += size
    copies = copy_all(pairs, in_sem)

    def fetch(src, start, s, k):
        rows = pl.ds(pl.multiple_of(start, 256), 256)
        at = n * nparts + s * 8 + k
        return pltpu.make_async_copy(src.at[rows], bbuf.at[pl.ds((s * 8 + k) * 256, 256)], in_sem.at[at])

    for s, delta in enumerate(deltas):
        zs = (z + delta) & (NZ - 1)
        at = zs * 256
        low = zs < NZ // 2
        whole = [
            fetch(right, at, s, 0),
            fetch(right, RIGHT_ROWS + at, s, 1),
            fetch(in1, RIGHT_ROWS - QUARTER + at, s, 3),
            fetch(out1, at, s, 4),
            fetch(in2, QUARTER + at, s, 6),
            fetch(out2, QUARTER + at, s, 7),
        ]
        near = (zs & 3) * 256
        first_half = [fetch(in2, near, s, 2), fetch(out1, RIGHT_ROWS + near, s, 5)]
        second_half = [fetch(in1, near, s, 2), fetch(out2, near, s, 5)]
        for copy in whole:
            copy.start()

        @pl.when(low)
        def _(chosen=first_half):
            for copy in chosen:
                copy.start()

        @pl.when(jnp.logical_not(low))
        def _(chosen=second_half):
            for copy in chosen:
                copy.start()

        copies = copies + whole + first_half

    if first:
        acc[...] = jnp.zeros_like(acc)
    else:
        acc[pl.ds(0, 64 * TILE)] = c_in[...]

    count = jnp.int32(0)
    for s, delta in enumerate(deltas):
        zs = (z + delta) & (NZ - 1)
        ra = slot(gid(zs, c, 1 - l, h) ^ me)

        def panel(k, count, s=s, zs=zs, ra=ra):
            at = k >> 1
            b_l = l ^ ((at ^ (at >> 1)) & 1)
            b_c = c ^ (k & 1)
            b = b_l * 2 + b_c
            rb = slot(gid(z, h ^ (at >> 1), b_l, b_c) ^ me)
            half = (h ^ (at >> 1) ^ c) * 32
            base = 32 + (zs * 2 + c) * 4
            live_a = meta[ra, b * 8 + 6]
            live_b = meta[rb, base + 2]
            ta = s * tiles + b * SA
            tb = s * 16 + k * 2
            for q in range(SB):
                place = meta[rb, base + q]
                for t in range(SA):
                    index = meta[ra, b * 8 + t]
                    i = index >> 3
                    chunk = ((i >> 2) - y) & 3
                    spot = chunk ^ (chunk >> 1)
                    block = half + (spot * 4 + (i & 3)) * 2 + (place & 1)
                    hit = ((index & 7) == (place >> 1)) & (t < live_a) & (q < live_b)
                    work[count] = (block << 20) | ((tb + q) << 10) | (ta + t)
                    count = count + hit.astype(jnp.int32)
            return count

        count = lax.fori_loop(0, 8, panel, count)
    for k in range(3):
        work[count + k] = jnp.int32(64 << 20)

    for copy in copies:
        copy.wait()

    def rows_of(k):
        return pl.ds(pl.multiple_of(k * TILE, TILE), TILE)

    def products(g, carry):
        for k in range(4):
            w = work[g * 4 + k]
            block = rows_of(w >> 20)
            acc[block] = acc[block] + jnp.dot(
                abuf[rows_of(w & 1023)], bbuf[rows_of((w >> 10) & 1023)], preferred_element_type=jnp.float32
            )
        return carry

    lax.fori_loop(0, (count + 3) >> 2, products, 0)

    for (start, size), out in zip(outs_rows, outs):
        out[...] = acc[pl.ds(start * TILE, size * TILE)]


def multiply(deltas, parts, tiles, ids, meta, lefts, rights, total, outs_rows):
    n = len(deltas)
    first = total is None
    operands = [ids, meta, *lefts, *rights] + ([] if first else [total])
    return pl.pallas_call(
        functools.partial(kernel, deltas, parts, tiles, first, outs_rows),
        out_shape=[jax.ShapeDtypeStruct((k * TILE, TILE), jnp.float32) for _, k in outs_rows],
        in_specs=[SMEM, SMEM] + [HBM] * (len(lefts) + 5) + ([] if first else [VMEM]),
        out_specs=[VMEM] * len(outs_rows),
        scratch_shapes=[
            pltpu.VMEM((n * tiles * TILE, TILE), jnp.bfloat16),
            pltpu.VMEM((n * 16 * TILE, TILE), jnp.bfloat16),
            pltpu.VMEM((65 * TILE, TILE), jnp.float32),
            pltpu.SMEM((n * 96 + 8,), jnp.int32),
            pltpu.SemaphoreType.DMA((len(lefts) + 8 * n,)),
        ],
        compiler_params=pltpu.CompilerParams(vmem_limit_bytes=(24 + 2 * n) * 1024 * 1024),
        cost_estimate=pl.CostEstimate(
            flops=n * 40_000_000, bytes_accessed=8_000_000 + n * 4_000_000, transcendentals=0
        ),
        name="products_%s" % "_".join(str(d & 7) for d in deltas),
    )(*operands)


send = lax.ppermute
barrier = lax.optimization_barrier


def onward(f, b):
    return send(f, "row", z_route(1)), send(b, "row", z_route(-1))


def inner(x):
    return send(x, "col", INNER_ROUTE)


def outer(x):
    return send(x, BOTH, outer_route())


REST = 2 * RIGHT_ROWS - QUARTER


def spread(meta, bit):
    return jnp.concatenate([meta, send(meta, BOTH, [(i, i ^ (1 << bit)) for i in range(64)])], axis=0)


def shards(a_tiles, a_index, a_count, b_tiles, b_place, b_count):
    row = lax.axis_index("row")
    col = lax.axis_index("col")
    y = lax.axis_index("depth")
    core = col & 1
    ids = jnp.stack([row >> 1, row & 1, col >> 1, core, y, y, y, y]).astype(jnp.int32)

    own = send(a_tiles.reshape(LEFT_ROWS, TILE), BOTH, swap_route())
    tiles = b_tiles.reshape(NZ, 2, SB * TILE, TILE)
    mine = lax.dynamic_index_in_dim(tiles, core, 1, keepdims=False).reshape(RIGHT_ROWS, TILE)
    theirs = lax.dynamic_index_in_dim(tiles, 1 - core, 1, keepdims=False).reshape(RIGHT_ROWS, TILE)
    right = jnp.concatenate([mine, send(theirs, "col", CORE_ROUTE)], axis=0)
    left_meta = jnp.pad(a_index.reshape(PANELS, SA), ((0, 0), (0, 2))) + jnp.pad(
        a_count.reshape(PANELS, 1), ((0, 0), (6, 1))
    )
    right_meta = jnp.pad(b_place.reshape(16, SB), ((0, 0), (0, 2))) + jnp.pad(
        b_count.reshape(16, 1), ((0, 0), (2, 1))
    )
    meta = jnp.concatenate(
        [left_meta.reshape(1, 32), right_meta.reshape(1, 64), jnp.zeros((1, 32), jnp.int32)], axis=1
    )
    around = [send(meta, BOTH, [(i, i ^ (k << 3)) for i in range(64)]) for k in (1, 2, 3)]
    meta = jnp.concatenate([meta, *around], axis=0)
    own, meta = barrier((own, meta))

    f1, b1 = onward(own, own)
    meta = spread(meta, BITS[2])
    right, meta = barrier((right, meta))
    in1, out1 = inner(right[QUARTER:]), outer(right[:REST])
    meta = spread(meta, BITS[3])
    f1, b1 = barrier((f1, b1))

    f2, b2 = onward(f1, b1)
    in1, out1, meta = barrier((in1, out1, meta))
    meta = spread(meta, BITS[4])
    in2 = jnp.concatenate([right[:QUARTER], out1[:RIGHT_ROWS]], axis=0)
    out2 = jnp.concatenate([right[REST:], in1[RIGHT_ROWS - QUARTER :]], axis=0)
    in2, out2, meta = barrier((in2, out2, meta))
    in2, out2 = inner(in2), outer(out2)
    meta = spread(meta, BITS[5])
    f2, b2, meta = barrier((f2, b2, meta))

    f3, b3 = onward(f2, b2)
    rights = [right, in1, in2, out1, out2]
    near = LEFT_ROWS // 2
    one = ((0, LEFT_ROWS),)
    two = ((0, near), (0, LEFT_ROWS - near))
    whole = ((0, 64),)
    (total,) = multiply(
        (0, -1, 1, -2, 2), one, ATILES, ids, meta, [own, f1, b1, f2, b2], rights, None, whole
    )
    f3, b3, total = barrier((f3, b3, total))
    far = [send(f3[:near], "row", z_route(1)), send(b3[near:], "row", z_route(-1))]
    (total,) = multiply((-3, 3), one, ATILES, ids, meta, [f3, b3], rights, total, whole)
    kept, other = multiply((4,), two, ATILES, ids, meta, far, rights, total, ((0, 32), (32, 32)))

    other = send(other, "col", CORE_ROUTE)
    half = 4 * TILE

    def unit(k, count=1):
        rows = slice(k * half, (k + count) * half)
        return kept[rows] + other[rows]

    units = barrier((unit(6), unit(7), unit(3), unit(4)))
    up2 = send(units[0], "depth", y_route(1))
    down2 = send(units[1], "depth", y_route(-1))
    up1 = send(units[2], ALL, home_route(1))
    down1 = send(units[3], ALL, home_route(-1))
    still = send(unit(0, 2), BOTH, swap_route())
    up2, down2 = barrier((up2, down2))
    up3 = send(unit(2) + up2, ALL, home_route(1))
    down3 = send(unit(5) + down2, ALL, home_route(-1))
    low = still[:half] + down1 + up3
    high = still[half:] + up1 + down3
    return jnp.concatenate([low, high], axis=0).reshape(4, 2, TILE, TILE)


def solution(mesh):
    placed = (
        P("row", "col", "depth", None, None, None, None),
        P("row", "col", "depth", None, None),
        P("row", "col", "depth", None),
        P("row", "col", "depth", None, None, None, None),
        P("row", "col", "depth", None, None),
        P("row", "col", "depth", None),
    )
    return jax.shard_map(
        shards,
        mesh=mesh,
        in_specs=placed,
        out_specs=P(("col", "depth"), "row", None, None),
        check_vma=False,
    )
```

```python
import functools

import jax
import jax.numpy as jnp
from jax import lax
from jax.experimental import pallas as pl
from jax.experimental.pallas import tpu as pltpu
from jax.sharding import PartitionSpec as P

NZ = 8
SA = 6
SB = 2
PANELS = 4
ATILES = PANELS * SA
TILE = 128
LEFT_ROWS = ATILES * TILE
RIGHT_ROWS = 8 * SB * TILE
QUARTER = 1024
BOTH = ("row", "col")
ALL = ("row", "col", "depth")
HBM = pl.BlockSpec(memory_space=pltpu.HBM)
VMEM = pl.BlockSpec(memory_space=pltpu.VMEM)
SMEM = pl.BlockSpec(memory_space=pltpu.SMEM)


def gid(z, h, l, c):
    return ((z * 2 + h) * 2 + l) * 2 + c


def group():
    return [(z, h, l, c) for z in range(NZ) for h in range(2) for l in range(2) for c in range(2)]


def swap_route():
    return [(gid(z, h, l, c), gid(z, c, 1 - l, h)) for z, h, l, c in group()]


def home_route(d):
    return [(s * 4 + y, t * 4 + (y + d) % 4) for s, t in swap_route() for y in range(4)]


def z_route(d):
    return [(2 * z + h, 2 * ((z + d) % NZ) + h) for z in range(NZ) for h in range(2)]


def y_route(d):
    return [(y, (y + d) % 4) for y in range(4)]


def outer_route():
    return [(gid(z, h, l, c), gid(z, 1 - h, 1 - l, c)) for z, h, l, c in group()]


BITS = (3, 4, 1, 2, 0, 5)


def slot(offset):
    return sum(((offset >> bit) & 1) << k for k, bit in enumerate(BITS))


CORE_ROUTE = [(i, i ^ 1) for i in range(4)]
INNER_ROUTE = [(i, i ^ 2) for i in range(4)]


def copy_all(pairs, sem):
    copies = []
    for src, dst in pairs:
        copy = pltpu.make_async_copy(src, dst, sem.at[len(copies)])
        copy.start()
        copies.append(copy)
    return copies


def kernel(deltas, parts, tiles, first, outs_rows, *refs):
    n = len(deltas)
    nparts = len(parts)
    refs = list(refs)

    def take(k):
        got = refs[:k]
        del refs[:k]
        return got

    ids, meta = take(2)
    lefts = take(n * nparts)
    right, in1, in2, out1, out2 = take(5)
    c_in = None if first else take(1)[0]
    outs = take(len(outs_rows))
    abuf, bbuf, acc, work, in_sem = refs

    z, h, l, c, y = (ids[k] for k in range(5))
    me = gid(z, h, l, c)
    pairs = []
    for s in range(n):
        spot = s * tiles * TILE
        for p, (start, size) in enumerate(parts):
            pairs.append((lefts[s * nparts + p].at[pl.ds(start, size)], abuf.at[pl.ds(spot, size)]))
            spot += size
    copies = copy_all(pairs, in_sem)

    def fetch(src, start, s, k):
        rows = pl.ds(pl.multiple_of(start, 256), 256)
        at = n * nparts + s * 8 + k
        return pltpu.make_async_copy(src.at[rows], bbuf.at[pl.ds((s * 8 + k) * 256, 256)], in_sem.at[at])

    for s, delta in enumerate(deltas):
        zs = (z + delta) & (NZ - 1)
        at = zs * 256
        low = zs < NZ // 2
        whole = [
            fetch(right, at, s, 0),
            fetch(right, RIGHT_ROWS + at, s, 1),
            fetch(in1, RIGHT_ROWS - QUARTER + at, s, 3),
            fetch(out1, at, s, 4),
            fetch(in2, QUARTER + at, s, 6),
            fetch(out2, QUARTER + at, s, 7),
        ]
        near = (zs & 3) * 256
        first_half = [fetch(in2, near, s, 2), fetch(out1, RIGHT_ROWS + near, s, 5)]
        second_half = [fetch(in1, near, s, 2), fetch(out2, near, s, 5)]
        for copy in whole:
            copy.start()

        @pl.when(low)
        def _(chosen=first_half):
            for copy in chosen:
                copy.start()

        @pl.when(jnp.logical_not(low))
        def _(chosen=second_half):
            for copy in chosen:
                copy.start()

        copies = copies + whole + first_half

    if first:
        acc[...] = jnp.zeros_like(acc)
    else:
        acc[pl.ds(0, 64 * TILE)] = c_in[...]

    count = jnp.int32(0)
    for s, delta in enumerate(deltas):
        zs = (z + delta) & (NZ - 1)
        ra = slot(gid(zs, c, 1 - l, h) ^ me)

        def panel(k, count, s=s, zs=zs, ra=ra):
            at = k >> 1
            b_l = l ^ ((at ^ (at >> 1)) & 1)
            b_c = c ^ (k & 1)
            b = b_l * 2 + b_c
            rb = slot(gid(z, h ^ (at >> 1), b_l, b_c) ^ me)
            half = (h ^ (at >> 1) ^ c) * 32
            base = 32 + (zs * 2 + c) * 4
            live_a = meta[ra, b * 8 + 6]
            live_b = meta[rb, base + 2]
            ta = s * tiles + b * SA
            tb = s * 16 + k * 2
            for q in range(SB):
                place = meta[rb, base + q]
                for t in range(SA):
                    index = meta[ra, b * 8 + t]
                    i = index >> 3
                    chunk = ((i >> 2) - y) & 3
                    spot = chunk ^ (chunk >> 1)
                    block = half + (spot * 4 + (i & 3)) * 2 + (place & 1)
                    hit = ((index & 7) == (place >> 1)) & (t < live_a) & (q < live_b)
                    work[count] = (block << 20) | ((tb + q) << 10) | (ta + t)
                    count = count + hit.astype(jnp.int32)
            return count

        count = lax.fori_loop(0, 8, panel, count)
    for k in range(3):
        work[count + k] = jnp.int32(64 << 20)

    for copy in copies:
        copy.wait()

    def rows_of(k):
        return pl.ds(pl.multiple_of(k * TILE, TILE), TILE)

    def products(g, carry):
        for k in range(4):
            w = work[g * 4 + k]
            block = rows_of(w >> 20)
            acc[block] = acc[block] + jnp.dot(
                abuf[rows_of(w & 1023)], bbuf[rows_of((w >> 10) & 1023)], preferred_element_type=jnp.float32
            )
        return carry

    lax.fori_loop(0, (count + 3) >> 2, products, 0)

    for (start, size), out in zip(outs_rows, outs):
        out[...] = acc[pl.ds(start * TILE, size * TILE)]


def multiply(deltas, parts, tiles, ids, meta, lefts, rights, total, outs_rows):
    n = len(deltas)
    first = total is None
    operands = [ids, meta, *lefts, *rights] + ([] if first else [total])
    return pl.pallas_call(
        functools.partial(kernel, deltas, parts, tiles, first, outs_rows),
        out_shape=[jax.ShapeDtypeStruct((k * TILE, TILE), jnp.float32) for _, k in outs_rows],
        in_specs=[SMEM, SMEM] + [HBM] * (len(lefts) + 5) + ([] if first else [VMEM]),
        out_specs=[VMEM] * len(outs_rows),
        scratch_shapes=[
            pltpu.VMEM((n * tiles * TILE, TILE), jnp.bfloat16),
            pltpu.VMEM((n * 16 * TILE, TILE), jnp.bfloat16),
            pltpu.VMEM((65 * TILE, TILE), jnp.float32),
            pltpu.SMEM((n * 96 + 8,), jnp.int32),
            pltpu.SemaphoreType.DMA((len(lefts) + 8 * n,)),
        ],
        compiler_params=pltpu.CompilerParams(vmem_limit_bytes=(24 + 2 * n) * 1024 * 1024),
        cost_estimate=pl.CostEstimate(
            flops=n * 40_000_000, bytes_accessed=8_000_000 + n * 4_000_000, transcendentals=0
        ),
        name="products_%s" % "_".join(str(d & 7) for d in deltas),
    )(*operands)


send = lax.ppermute
barrier = lax.optimization_barrier


def onward(f, b):
    return send(f, "row", z_route(1)), send(b, "row", z_route(-1))


def inner(x):
    return send(x, "col", INNER_ROUTE)


def outer(x):
    return send(x, BOTH, outer_route())


REST = 2 * RIGHT_ROWS - QUARTER


def spread_two(meta, low):
    around = [send(meta, BOTH, [(i, i ^ (k << low)) for i in range(64)]) for k in (1, 2, 3)]
    return jnp.concatenate([meta, *around], axis=0)


def spread(meta, bit):
    return jnp.concatenate([meta, send(meta, BOTH, [(i, i ^ (1 << bit)) for i in range(64)])], axis=0)


def shards(a_tiles, a_index, a_count, b_tiles, b_place, b_count):
    row = lax.axis_index("row")
    col = lax.axis_index("col")
    y = lax.axis_index("depth")
    core = col & 1
    ids = jnp.stack([row >> 1, row & 1, col >> 1, core, y, y, y, y]).astype(jnp.int32)

    own = send(a_tiles.reshape(LEFT_ROWS, TILE), BOTH, swap_route())
    tiles = b_tiles.reshape(NZ, 2, SB * TILE, TILE)
    mine = lax.dynamic_index_in_dim(tiles, core, 1, keepdims=False).reshape(RIGHT_ROWS, TILE)
    theirs = lax.dynamic_index_in_dim(tiles, 1 - core, 1, keepdims=False).reshape(RIGHT_ROWS, TILE)
    right = jnp.concatenate([mine, send(theirs, "col", CORE_ROUTE)], axis=0)
    left_meta = jnp.pad(a_index.reshape(PANELS, SA), ((0, 0), (0, 2))) + jnp.pad(
        a_count.reshape(PANELS, 1), ((0, 0), (6, 1))
    )
    right_meta = jnp.pad(b_place.reshape(16, SB), ((0, 0), (0, 2))) + jnp.pad(
        b_count.reshape(16, 1), ((0, 0), (2, 1))
    )
    meta = jnp.concatenate(
        [left_meta.reshape(1, 32), right_meta.reshape(1, 64), jnp.zeros((1, 32), jnp.int32)], axis=1
    )
    meta = spread_two(meta, 3)
    own, meta = barrier((own, meta))

    f1, b1 = onward(own, own)
    meta = spread_two(meta, 1)
    right, meta = barrier((right, meta))
    in1, out1 = inner(right[QUARTER:]), outer(right[:REST])
    meta = spread(spread(meta, BITS[4]), BITS[5])
    f1, b1, meta = barrier((f1, b1, meta))

    f2, b2 = onward(f1, b1)
    in2 = jnp.concatenate([right[:QUARTER], out1[:RIGHT_ROWS]], axis=0)
    out2 = jnp.concatenate([right[REST:], in1[RIGHT_ROWS - QUARTER :]], axis=0)
    in2, out2 = inner(in2), outer(out2)
    f2, b2 = barrier((f2, b2))

    f3, b3 = onward(f2, b2)
    rights = [right, in1, in2, out1, out2]
    near = LEFT_ROWS // 2
    one = ((0, LEFT_ROWS),)
    two = ((0, near), (0, LEFT_ROWS - near))
    whole = ((0, 64),)
    (total,) = multiply((0, -1, 1), one, ATILES, ids, meta, [own, f1, b1], rights, None, whole)
    f3, b3, total = barrier((f3, b3, total))
    far = [send(f3[:near], "row", z_route(1)), send(b3[near:], "row", z_route(-1))]
    (total,) = multiply((-2, 2, -3, 3), one, ATILES, ids, meta, [f2, b2, f3, b3], rights, total, whole)
    kept, other = multiply((4,), two, ATILES, ids, meta, far, rights, total, ((0, 32), (32, 32)))

    other = send(other, "col", CORE_ROUTE)
    half = 4 * TILE

    def unit(k, count=1):
        rows = slice(k * half, (k + count) * half)
        return kept[rows] + other[rows]

    units = barrier((unit(6), unit(7), unit(3), unit(4)))
    up2 = send(units[0], "depth", y_route(1))
    down2 = send(units[1], "depth", y_route(-1))
    up1 = send(units[2], ALL, home_route(1))
    down1 = send(units[3], ALL, home_route(-1))
    still = send(unit(0, 2), BOTH, swap_route())
    up2, down2 = barrier((up2, down2))
    up3 = send(unit(2) + up2, ALL, home_route(1))
    down3 = send(unit(5) + down2, ALL, home_route(-1))
    low = still[:half] + down1 + up3
    high = still[half:] + up1 + down3
    return jnp.concatenate([low, high], axis=0).reshape(4, 2, TILE, TILE)


def solution(mesh):
    placed = (
        P("row", "col", "depth", None, None, None, None),
        P("row", "col", "depth", None, None),
        P("row", "col", "depth", None),
        P("row", "col", "depth", None, None, None, None),
        P("row", "col", "depth", None, None),
        P("row", "col", "depth", None),
    )
    return jax.shard_map(
        shards,
        mesh=mesh,
        in_specs=placed,
        out_specs=P(("col", "depth"), "row", None, None),
        check_vma=False,
    )
```

```python
import functools

import jax
import jax.numpy as jnp
from jax import lax
from jax.experimental import pallas as pl
from jax.experimental.pallas import tpu as pltpu
from jax.sharding import PartitionSpec as P

NZ = 8
SA = 6
SB = 2
PANELS = 4
ATILES = PANELS * SA
TILE = 128
LEFT_ROWS = ATILES * TILE
RIGHT_ROWS = 8 * SB * TILE
QUARTER = 1024
BOTH = ("row", "col")
ALL = ("row", "col", "depth")
HBM = pl.BlockSpec(memory_space=pltpu.HBM)
VMEM = pl.BlockSpec(memory_space=pltpu.VMEM)
SMEM = pl.BlockSpec(memory_space=pltpu.SMEM)


def gid(z, h, l, c):
    return ((z * 2 + h) * 2 + l) * 2 + c


def group():
    return [(z, h, l, c) for z in range(NZ) for h in range(2) for l in range(2) for c in range(2)]


def swap_route():
    return [(gid(z, h, l, c), gid(z, c, 1 - l, h)) for z, h, l, c in group()]


def home_route(d):
    return [(s * 4 + y, t * 4 + (y + d) % 4) for s, t in swap_route() for y in range(4)]


def z_route(d):
    return [(2 * z + h, 2 * ((z + d) % NZ) + h) for z in range(NZ) for h in range(2)]


def y_route(d):
    return [(y, (y + d) % 4) for y in range(4)]


def outer_route():
    return [(gid(z, h, l, c), gid(z, 1 - h, 1 - l, c)) for z, h, l, c in group()]


BITS = (3, 4, 1, 2, 0, 5)


def slot(offset):
    return sum(((offset >> bit) & 1) << k for k, bit in enumerate(BITS))


CORE_ROUTE = [(i, i ^ 1) for i in range(4)]
INNER_ROUTE = [(i, i ^ 2) for i in range(4)]


def copy_all(pairs, sem):
    copies = []
    for src, dst in pairs:
        copy = pltpu.make_async_copy(src, dst, sem.at[len(copies)])
        copy.start()
        copies.append(copy)
    return copies


def kernel(deltas, parts, tiles, first, outs_rows, *refs):
    n = len(deltas)
    nparts = len(parts)
    refs = list(refs)

    def take(k):
        got = refs[:k]
        del refs[:k]
        return got

    ids, meta = take(2)
    lefts = take(n * nparts)
    right, in1, in2, out1, out2 = take(5)
    c_in = None if first else take(1)[0]
    outs = take(len(outs_rows))
    abuf, bbuf, acc, work, in_sem = refs

    z, h, l, c, y = (ids[k] for k in range(5))
    me = gid(z, h, l, c)
    pairs = []
    for s in range(n):
        spot = s * tiles * TILE
        for p, (start, size) in enumerate(parts):
            pairs.append((lefts[s * nparts + p].at[pl.ds(start, size)], abuf.at[pl.ds(spot, size)]))
            spot += size
    copies = copy_all(pairs, in_sem)

    def fetch(src, start, s, k):
        rows = pl.ds(pl.multiple_of(start, 256), 256)
        at = n * nparts + s * 8 + k
        return pltpu.make_async_copy(src.at[rows], bbuf.at[pl.ds((s * 8 + k) * 256, 256)], in_sem.at[at])

    for s, delta in enumerate(deltas):
        zs = (z + delta) & (NZ - 1)
        at = zs * 256
        low = zs < NZ // 2
        whole = [
            fetch(right, at, s, 0),
            fetch(right, RIGHT_ROWS + at, s, 1),
            fetch(in1, RIGHT_ROWS - QUARTER + at, s, 3),
            fetch(out1, at, s, 4),
            fetch(in2, QUARTER + at, s, 6),
            fetch(out2, QUARTER + at, s, 7),
        ]
        near = (zs & 3) * 256
        first_half = [fetch(in2, near, s, 2), fetch(out1, RIGHT_ROWS + near, s, 5)]
        second_half = [fetch(in1, near, s, 2), fetch(out2, near, s, 5)]
        for copy in whole:
            copy.start()

        @pl.when(low)
        def _(chosen=first_half):
            for copy in chosen:
                copy.start()

        @pl.when(jnp.logical_not(low))
        def _(chosen=second_half):
            for copy in chosen:
                copy.start()

        copies = copies + whole + first_half

    if first:
        acc[...] = jnp.zeros_like(acc)
    else:
        acc[pl.ds(0, 64 * TILE)] = c_in[...]

    count = jnp.int32(0)
    for s, delta in enumerate(deltas):
        zs = (z + delta) & (NZ - 1)
        ra = slot(gid(zs, c, 1 - l, h) ^ me)

        def panel(k, count, s=s, zs=zs, ra=ra):
            at = k >> 1
            b_l = l ^ ((at ^ (at >> 1)) & 1)
            b_c = c ^ (k & 1)
            b = b_l * 2 + b_c
            rb = slot(gid(z, h ^ (at >> 1), b_l, b_c) ^ me)
            half = (h ^ (at >> 1) ^ c) * 32
            base = 32 + (zs * 2 + c) * 4
            live_a = meta[ra, b * 8 + 6]
            live_b = meta[rb, base + 2]
            ta = s * tiles + b * SA
            tb = s * 16 + k * 2
            for q in range(SB):
                place = meta[rb, base + q]
                for t in range(SA):
                    index = meta[ra, b * 8 + t]
                    i = index >> 3
                    chunk = ((i >> 2) - y) & 3
                    spot = chunk ^ (chunk >> 1)
                    block = half + (spot * 4 + (i & 3)) * 2 + (place & 1)
                    hit = ((index & 7) == (place >> 1)) & (t < live_a) & (q < live_b)
                    work[count] = (block << 20) | ((tb + q) << 10) | (ta + t)
                    count = count + hit.astype(jnp.int32)
            return count

        count = lax.fori_loop(0, 8, panel, count)
    for k in range(3):
        work[count + k] = jnp.int32(64 << 20)

    for copy in copies:
        copy.wait()

    def rows_of(k):
        return pl.ds(pl.multiple_of(k * TILE, TILE), TILE)

    def products(g, carry):
        for k in range(4):
            w = work[g * 4 + k]
            block = rows_of(w >> 20)
            acc[block] = acc[block] + jnp.dot(
                abuf[rows_of(w & 1023)], bbuf[rows_of((w >> 10) & 1023)], preferred_element_type=jnp.float32
            )
        return carry

    lax.fori_loop(0, (count + 3) >> 2, products, 0)

    for (start, size), out in zip(outs_rows, outs):
        out[...] = acc[pl.ds(start * TILE, size * TILE)]


def multiply(deltas, parts, tiles, ids, meta, lefts, rights, total, outs_rows):
    n = len(deltas)
    first = total is None
    operands = [ids, meta, *lefts, *rights] + ([] if first else [total])
    return pl.pallas_call(
        functools.partial(kernel, deltas, parts, tiles, first, outs_rows),
        out_shape=[jax.ShapeDtypeStruct((k * TILE, TILE), jnp.float32) for _, k in outs_rows],
        in_specs=[SMEM, SMEM] + [HBM] * (len(lefts) + 5) + ([] if first else [VMEM]),
        out_specs=[VMEM] * len(outs_rows),
        scratch_shapes=[
            pltpu.VMEM((n * tiles * TILE, TILE), jnp.bfloat16),
            pltpu.VMEM((n * 16 * TILE, TILE), jnp.bfloat16),
            pltpu.VMEM((65 * TILE, TILE), jnp.float32),
            pltpu.SMEM((n * 96 + 8,), jnp.int32),
            pltpu.SemaphoreType.DMA((len(lefts) + 8 * n,)),
        ],
        compiler_params=pltpu.CompilerParams(vmem_limit_bytes=(24 + 2 * n) * 1024 * 1024),
        cost_estimate=pl.CostEstimate(
            flops=n * 40_000_000, bytes_accessed=8_000_000 + n * 4_000_000, transcendentals=0
        ),
        name="products_%s" % "_".join(str(d & 7) for d in deltas),
    )(*operands)


send = lax.ppermute
barrier = lax.optimization_barrier


def onward(f, b):
    return send(f, "row", z_route(1)), send(b, "row", z_route(-1))


def inner(x):
    return send(x, "col", INNER_ROUTE)


def outer(x):
    return send(x, BOTH, outer_route())


REST = 2 * RIGHT_ROWS - QUARTER


def spread_two(meta, low):
    around = [send(meta, BOTH, [(i, i ^ (k << low)) for i in range(64)]) for k in (1, 2, 3)]
    return jnp.concatenate([meta, *around], axis=0)


def spread(meta, bit):
    return jnp.concatenate([meta, send(meta, BOTH, [(i, i ^ (1 << bit)) for i in range(64)])], axis=0)


def shards(a_tiles, a_index, a_count, b_tiles, b_place, b_count):
    row = lax.axis_index("row")
    col = lax.axis_index("col")
    y = lax.axis_index("depth")
    core = col & 1
    ids = jnp.stack([row >> 1, row & 1, col >> 1, core, y, y, y, y]).astype(jnp.int32)

    own = send(a_tiles.reshape(LEFT_ROWS, TILE), BOTH, swap_route())
    tiles = b_tiles.reshape(NZ, 2, SB * TILE, TILE)
    mine = lax.dynamic_index_in_dim(tiles, core, 1, keepdims=False).reshape(RIGHT_ROWS, TILE)
    theirs = lax.dynamic_index_in_dim(tiles, 1 - core, 1, keepdims=False).reshape(RIGHT_ROWS, TILE)
    right = jnp.concatenate([mine, send(theirs, "col", CORE_ROUTE)], axis=0)
    left_meta = jnp.pad(a_index.reshape(PANELS, SA), ((0, 0), (0, 2))) + jnp.pad(
        a_count.reshape(PANELS, 1), ((0, 0), (6, 1))
    )
    right_meta = jnp.pad(b_place.reshape(16, SB), ((0, 0), (0, 2))) + jnp.pad(
        b_count.reshape(16, 1), ((0, 0), (2, 1))
    )
    meta = jnp.concatenate(
        [left_meta.reshape(1, 32), right_meta.reshape(1, 64), jnp.zeros((1, 32), jnp.int32)], axis=1
    )
    meta = spread_two(spread_two(meta, 3), 1)
    own, right, meta = barrier((own, right, meta))

    f1, b1 = onward(own, own)
    in1, out1 = inner(right[QUARTER:]), outer(right[:REST])
    meta = spread(spread(meta, BITS[4]), BITS[5])
    f1, b1, meta = barrier((f1, b1, meta))

    f2, b2 = onward(f1, b1)
    in2 = jnp.concatenate([right[:QUARTER], out1[:RIGHT_ROWS]], axis=0)
    out2 = jnp.concatenate([right[REST:], in1[RIGHT_ROWS - QUARTER :]], axis=0)
    in2, out2 = inner(in2), outer(out2)
    f2, b2 = barrier((f2, b2))

    f3, b3 = onward(f2, b2)
    rights = [right, in1, in2, out1, out2]
    near = LEFT_ROWS // 2
    one = ((0, LEFT_ROWS),)
    two = ((0, near), (0, LEFT_ROWS - near))
    whole = ((0, 64),)
    (total,) = multiply((0, -1, 1), one, ATILES, ids, meta, [own, f1, b1], rights, None, whole)
    f3, b3, total = barrier((f3, b3, total))
    far = [send(f3[:near], "row", z_route(1)), send(b3[near:], "row", z_route(-1))]
    (total,) = multiply((-2, 2, -3, 3), one, ATILES, ids, meta, [f2, b2, f3, b3], rights, total, whole)
    kept, other = multiply((4,), two, ATILES, ids, meta, far, rights, total, ((0, 32), (32, 32)))

    other = send(other, "col", CORE_ROUTE)
    half = 4 * TILE

    def unit(k, count=1):
        rows = slice(k * half, (k + count) * half)
        return kept[rows] + other[rows]

    units = barrier((unit(6), unit(7), unit(3), unit(4)))
    up2 = send(units[0], "depth", y_route(1))
    down2 = send(units[1], "depth", y_route(-1))
    up1 = send(units[2], ALL, home_route(1))
    down1 = send(units[3], ALL, home_route(-1))
    still = send(unit(0, 2), BOTH, swap_route())
    up2, down2 = barrier((up2, down2))
    up3 = send(unit(2) + up2, ALL, home_route(1))
    down3 = send(unit(5) + down2, ALL, home_route(-1))
    low = still[:half] + down1 + up3
    high = still[half:] + up1 + down3
    return jnp.concatenate([low, high], axis=0).reshape(4, 2, TILE, TILE)


def solution(mesh):
    placed = (
        P("row", "col", "depth", None, None, None, None),
        P("row", "col", "depth", None, None),
        P("row", "col", "depth", None),
        P("row", "col", "depth", None, None, None, None),
        P("row", "col", "depth", None, None),
        P("row", "col", "depth", None),
    )
    return jax.shard_map(
        shards,
        mesh=mesh,
        in_specs=placed,
        out_specs=P(("col", "depth"), "row", None, None),
        check_vma=False,
    )
```

```python
import functools

import jax
import jax.numpy as jnp
from jax import lax
from jax.experimental import pallas as pl
from jax.experimental.pallas import tpu as pltpu
from jax.sharding import PartitionSpec as P

NZ = 8
SA = 6
SB = 2
PANELS = 4
ATILES = PANELS * SA
TILE = 128
LEFT_ROWS = ATILES * TILE
RIGHT_ROWS = 8 * SB * TILE
QUARTER = 1024
BOTH = ("row", "col")
ALL = ("row", "col", "depth")
HBM = pl.BlockSpec(memory_space=pltpu.HBM)
VMEM = pl.BlockSpec(memory_space=pltpu.VMEM)
SMEM = pl.BlockSpec(memory_space=pltpu.SMEM)


def gid(z, h, l, c):
    return ((z * 2 + h) * 2 + l) * 2 + c


def group():
    return [(z, h, l, c) for z in range(NZ) for h in range(2) for l in range(2) for c in range(2)]


def swap_route():
    return [(gid(z, h, l, c), gid(z, c, 1 - l, h)) for z, h, l, c in group()]


def home_route(d):
    return [(s * 4 + y, t * 4 + (y + d) % 4) for s, t in swap_route() for y in range(4)]


def z_route(d):
    return [(2 * z + h, 2 * ((z + d) % NZ) + h) for z in range(NZ) for h in range(2)]


def far_route():
    return [(gid(z, h, l, c), gid((z + 1 - 2 * c) % NZ, h, l, c)) for z, h, l, c in group()]


def y_route(d):
    return [(y, (y + d) % 4) for y in range(4)]


def outer_route():
    return [(gid(z, h, l, c), gid(z, 1 - h, 1 - l, c)) for z, h, l, c in group()]


BITS = (3, 4, 1, 2, 0, 5)


def slot(offset):
    return sum(((offset >> bit) & 1) << k for k, bit in enumerate(BITS))


CORE_ROUTE = [(i, i ^ 1) for i in range(4)]
INNER_ROUTE = [(i, i ^ 2) for i in range(4)]


def copy_all(pairs, sem):
    copies = []
    for src, dst in pairs:
        copy = pltpu.make_async_copy(src, dst, sem.at[len(copies)])
        copy.start()
        copies.append(copy)
    return copies


def kernel(deltas, parts, tiles, first, outs_rows, *refs):
    n = len(deltas)
    nparts = len(parts)
    refs = list(refs)

    def take(k):
        got = refs[:k]
        del refs[:k]
        return got

    ids, meta = take(2)
    lefts = take(n * nparts)
    right, in1, in2, out1, out2 = take(5)
    c_in = None if first else take(1)[0]
    outs = take(len(outs_rows))
    abuf, bbuf, acc, work, in_sem = refs

    z, h, l, c, y = (ids[k] for k in range(5))
    me = gid(z, h, l, c)
    pairs = []
    for s in range(n):
        spot = s * tiles * TILE
        for p, (start, size) in enumerate(parts):
            pairs.append((lefts[s * nparts + p].at[pl.ds(start, size)], abuf.at[pl.ds(spot, size)]))
            spot += size
    copies = copy_all(pairs, in_sem)

    def fetch(src, start, s, k):
        rows = pl.ds(pl.multiple_of(start, 256), 256)
        at = n * nparts + s * 8 + k
        return pltpu.make_async_copy(src.at[rows], bbuf.at[pl.ds((s * 8 + k) * 256, 256)], in_sem.at[at])

    for s, delta in enumerate(deltas):
        zs = (z + delta) & (NZ - 1)
        at = zs * 256
        low = zs < NZ // 2
        whole = [
            fetch(right, at, s, 0),
            fetch(right, RIGHT_ROWS + at, s, 1),
            fetch(in1, RIGHT_ROWS - QUARTER + at, s, 3),
            fetch(out1, at, s, 4),
            fetch(in2, QUARTER + at, s, 6),
            fetch(out2, QUARTER + at, s, 7),
        ]
        near = (zs & 3) * 256
        first_half = [fetch(in2, near, s, 2), fetch(out1, RIGHT_ROWS + near, s, 5)]
        second_half = [fetch(in1, near, s, 2), fetch(out2, near, s, 5)]
        for copy in whole:
            copy.start()

        @pl.when(low)
        def _(chosen=first_half):
            for copy in chosen:
                copy.start()

        @pl.when(jnp.logical_not(low))
        def _(chosen=second_half):
            for copy in chosen:
                copy.start()

        copies = copies + whole + first_half

    if first:
        acc[...] = jnp.zeros_like(acc)
    else:
        acc[pl.ds(0, 64 * TILE)] = c_in[...]

    count = jnp.int32(0)
    for s, delta in enumerate(deltas):
        zs = (z + delta) & (NZ - 1)
        ra = slot(gid(zs, c, 1 - l, h) ^ me)

        def panel(k, count, s=s, zs=zs, ra=ra):
            at = k >> 1
            b_l = l ^ ((at ^ (at >> 1)) & 1)
            b_c = c ^ (k & 1)
            b = b_l * 2 + b_c
            rb = slot(gid(z, h ^ (at >> 1), b_l, b_c) ^ me)
            half = (h ^ (at >> 1) ^ c) * 32
            base = 32 + (zs * 2 + c) * 4
            live_a = meta[ra, b * 8 + 6]
            live_b = meta[rb, base + 2]
            ta = s * tiles + b * SA
            tb = s * 16 + k * 2
            for q in range(SB):
                place = meta[rb, base + q]
                for t in range(SA):
                    index = meta[ra, b * 8 + t]
                    i = index >> 3
                    chunk = ((i >> 2) - y) & 3
                    spot = chunk ^ (chunk >> 1)
                    block = half + (spot * 4 + (i & 3)) * 2 + (place & 1)
                    hit = ((index & 7) == (place >> 1)) & (t < live_a) & (q < live_b)
                    work[count] = (block << 20) | ((tb + q) << 10) | (ta + t)
                    count = count + hit.astype(jnp.int32)
            return count

        count = lax.fori_loop(0, 8, panel, count)
    for k in range(3):
        work[count + k] = jnp.int32(64 << 20)

    for copy in copies:
        copy.wait()

    def rows_of(k):
        return pl.ds(pl.multiple_of(k * TILE, TILE), TILE)

    def products(g, carry):
        for k in range(4):
            w = work[g * 4 + k]
            block = rows_of(w >> 20)
            acc[block] = acc[block] + jnp.dot(
                abuf[rows_of(w & 1023)], bbuf[rows_of((w >> 10) & 1023)], preferred_element_type=jnp.float32
            )
        return carry

    lax.fori_loop(0, (count + 3) >> 2, products, 0)

    for (start, size), out in zip(outs_rows, outs):
        out[...] = acc[pl.ds(start * TILE, size * TILE)]


def multiply(deltas, parts, tiles, ids, meta, lefts, rights, total, outs_rows):
    n = len(deltas)
    first = total is None
    operands = [ids, meta, *lefts, *rights] + ([] if first else [total])
    return pl.pallas_call(
        functools.partial(kernel, deltas, parts, tiles, first, outs_rows),
        out_shape=[jax.ShapeDtypeStruct((k * TILE, TILE), jnp.float32) for _, k in outs_rows],
        in_specs=[SMEM, SMEM] + [HBM] * (len(lefts) + 5) + ([] if first else [VMEM]),
        out_specs=[VMEM] * len(outs_rows),
        scratch_shapes=[
            pltpu.VMEM((n * tiles * TILE, TILE), jnp.bfloat16),
            pltpu.VMEM((n * 16 * TILE, TILE), jnp.bfloat16),
            pltpu.VMEM((65 * TILE, TILE), jnp.float32),
            pltpu.SMEM((n * 96 + 8,), jnp.int32),
            pltpu.SemaphoreType.DMA((len(lefts) + 8 * n,)),
        ],
        compiler_params=pltpu.CompilerParams(vmem_limit_bytes=(24 + 2 * n) * 1024 * 1024),
        cost_estimate=pl.CostEstimate(
            flops=n * 40_000_000, bytes_accessed=8_000_000 + n * 4_000_000, transcendentals=0
        ),
        name="products_%s" % "_".join(str(d & 7) for d in deltas),
    )(*operands)


send = lax.ppermute
barrier = lax.optimization_barrier


def onward(f, b):
    return send(f, "row", z_route(1)), send(b, "row", z_route(-1))


def inner(x):
    return send(x, "col", INNER_ROUTE)


def outer(x):
    return send(x, BOTH, outer_route())


REST = 2 * RIGHT_ROWS - QUARTER


def spread_two(meta, low):
    around = [send(meta, BOTH, [(i, i ^ (k << low)) for i in range(64)]) for k in (1, 2, 3)]
    return jnp.concatenate([meta, *around], axis=0)


def spread(meta, bit):
    return jnp.concatenate([meta, send(meta, BOTH, [(i, i ^ (1 << bit)) for i in range(64)])], axis=0)


def shards(a_tiles, a_index, a_count, b_tiles, b_place, b_count):
    row = lax.axis_index("row")
    col = lax.axis_index("col")
    y = lax.axis_index("depth")
    core = col & 1
    ids = jnp.stack([row >> 1, row & 1, col >> 1, core, y, y, y, y]).astype(jnp.int32)

    own = send(a_tiles.reshape(LEFT_ROWS, TILE), BOTH, swap_route())
    tiles = b_tiles.reshape(NZ, 2, SB * TILE, TILE)
    mine = lax.dynamic_index_in_dim(tiles, core, 1, keepdims=False).reshape(RIGHT_ROWS, TILE)
    theirs = lax.dynamic_index_in_dim(tiles, 1 - core, 1, keepdims=False).reshape(RIGHT_ROWS, TILE)
    right = jnp.concatenate([mine, send(theirs, "col", CORE_ROUTE)], axis=0)
    left_meta = jnp.pad(a_index.reshape(PANELS, SA), ((0, 0), (0, 2))) + jnp.pad(
        a_count.reshape(PANELS, 1), ((0, 0), (6, 1))
    )
    right_meta = jnp.pad(b_place.reshape(16, SB), ((0, 0), (0, 2))) + jnp.pad(
        b_count.reshape(16, 1), ((0, 0), (2, 1))
    )
    meta = jnp.concatenate(
        [left_meta.reshape(1, 32), right_meta.reshape(1, 64), jnp.zeros((1, 32), jnp.int32)], axis=1
    )
    meta = spread_two(spread_two(meta, 3), 1)
    own, right, meta = barrier((own, right, meta))

    f1, b1 = onward(own, own)
    in1, out1 = inner(right[QUARTER:]), outer(right[:REST])
    meta = spread(spread(meta, BITS[4]), BITS[5])
    f1, b1, meta = barrier((f1, b1, meta))

    f2, b2 = onward(f1, b1)
    in2 = jnp.concatenate([right[:QUARTER], out1[:RIGHT_ROWS]], axis=0)
    out2 = jnp.concatenate([right[REST:], in1[RIGHT_ROWS - QUARTER :]], axis=0)
    in2, out2 = inner(in2), outer(out2)
    f2, b2 = barrier((f2, b2))

    f3, b3 = onward(f2, b2)
    rights = [right, in1, in2, out1, out2]
    one = ((0, LEFT_ROWS),)
    whole = ((0, 64),)
    (total,) = multiply((0, -1, 1), one, ATILES, ids, meta, [own, f1, b1], rights, None, whole)
    f3, b3, total = barrier((f3, b3, total))
    far = [send(jnp.where(core == 0, f3, b3), BOTH, far_route())]
    (total,) = multiply((-2, 2, -3, 3), one, ATILES, ids, meta, [f2, b2, f3, b3], rights, total, whole)
    kept, other = multiply((4,), one, ATILES, ids, meta, far, rights, total, ((0, 32), (32, 32)))

    other = send(other, "col", CORE_ROUTE)
    half = 4 * TILE

    def unit(k, count=1):
        rows = slice(k * half, (k + count) * half)
        return kept[rows] + other[rows]

    units = barrier((unit(6), unit(7), unit(3), unit(4)))
    up2 = send(units[0], "depth", y_route(1))
    down2 = send(units[1], "depth", y_route(-1))
    up1 = send(units[2], ALL, home_route(1))
    down1 = send(units[3], ALL, home_route(-1))
    still = send(unit(0, 2), BOTH, swap_route())
    up2, down2 = barrier((up2, down2))
    up3 = send(unit(2) + up2, ALL, home_route(1))
    down3 = send(unit(5) + down2, ALL, home_route(-1))
    low = still[:half] + down1 + up3
    high = still[half:] + up1 + down3
    return jnp.concatenate([low, high], axis=0).reshape(4, 2, TILE, TILE)


def solution(mesh):
    placed = (
        P("row", "col", "depth", None, None, None, None),
        P("row", "col", "depth", None, None),
        P("row", "col", "depth", None),
        P("row", "col", "depth", None, None, None, None),
        P("row", "col", "depth", None, None),
        P("row", "col", "depth", None),
    )
    return jax.shard_map(
        shards,
        mesh=mesh,
        in_specs=placed,
        out_specs=P(("col", "depth"), "row", None, None),
        check_vma=False,
    )
```

```python
import functools

import jax
import jax.numpy as jnp
from jax import lax
from jax.experimental import pallas as pl
from jax.experimental.pallas import tpu as pltpu
from jax.sharding import PartitionSpec as P

NZ = 8
SA = 6
SB = 2
PANELS = 4
ATILES = PANELS * SA
TILE = 128
LEFT_ROWS = ATILES * TILE
RIGHT_ROWS = 8 * SB * TILE
QUARTER = 1024
BOTH = ("row", "col")
ALL = ("row", "col", "depth")
HBM = pl.BlockSpec(memory_space=pltpu.HBM)
VMEM = pl.BlockSpec(memory_space=pltpu.VMEM)
SMEM = pl.BlockSpec(memory_space=pltpu.SMEM)


def gid(z, h, l, c):
    return ((z * 2 + h) * 2 + l) * 2 + c


def group():
    return [(z, h, l, c) for z in range(NZ) for h in range(2) for l in range(2) for c in range(2)]


def swap_route():
    return [(gid(z, h, l, c), gid(z, c, 1 - l, h)) for z, h, l, c in group()]


def home_route(d):
    return [(s * 4 + y, t * 4 + (y + d) % 4) for s, t in swap_route() for y in range(4)]


def z_route(d):
    return [(2 * z + h, 2 * ((z + d) % NZ) + h) for z in range(NZ) for h in range(2)]


def far_route():
    return [(gid(z, h, l, c), gid((z + 1 - 2 * c) % NZ, h, l, c)) for z, h, l, c in group()]


def y_route(d):
    return [(y, (y + d) % 4) for y in range(4)]


def outer_route():
    return [(gid(z, h, l, c), gid(z, 1 - h, 1 - l, c)) for z, h, l, c in group()]


BITS = (3, 4, 1, 2, 0, 5)


def slot(offset):
    return sum(((offset >> bit) & 1) << k for k, bit in enumerate(BITS))


CORE_ROUTE = [(i, i ^ 1) for i in range(4)]
INNER_ROUTE = [(i, i ^ 2) for i in range(4)]


def copy_all(pairs, sem):
    copies = []
    for src, dst in pairs:
        copy = pltpu.make_async_copy(src, dst, sem.at[len(copies)])
        copy.start()
        copies.append(copy)
    return copies


def kernel(deltas, parts, tiles, first, outs_rows, *refs):
    n = len(deltas)
    nparts = len(parts)
    refs = list(refs)

    def take(k):
        got = refs[:k]
        del refs[:k]
        return got

    ids, meta = take(2)
    lefts = take(n * nparts)
    right, in1, in2, out1, out2 = take(5)
    c_in = None if first else take(1)[0]
    outs = take(len(outs_rows))
    abuf, bbuf, acc, work, in_sem = refs

    z, h, l, c, y = (ids[k] for k in range(5))
    me = gid(z, h, l, c)
    pairs = []
    for s in range(n):
        spot = s * tiles * TILE
        for p, (start, size) in enumerate(parts):
            pairs.append((lefts[s * nparts + p].at[pl.ds(start, size)], abuf.at[pl.ds(spot, size)]))
            spot += size
    copies = copy_all(pairs, in_sem)

    def fetch(src, start, s, k):
        rows = pl.ds(pl.multiple_of(start, 256), 256)
        at = n * nparts + s * 8 + k
        return pltpu.make_async_copy(src.at[rows], bbuf.at[pl.ds((s * 8 + k) * 256, 256)], in_sem.at[at])

    for s, delta in enumerate(deltas):
        zs = (z + delta) & (NZ - 1)
        at = zs * 256
        low = zs < NZ // 2
        whole = [
            fetch(right, at, s, 0),
            fetch(right, RIGHT_ROWS + at, s, 1),
            fetch(in1, RIGHT_ROWS - QUARTER + at, s, 3),
            fetch(out1, at, s, 4),
            fetch(in2, QUARTER + at, s, 6),
            fetch(out2, QUARTER + at, s, 7),
        ]
        near = (zs & 3) * 256
        first_half = [fetch(in2, near, s, 2), fetch(out1, RIGHT_ROWS + near, s, 5)]
        second_half = [fetch(in1, near, s, 2), fetch(out2, near, s, 5)]
        for copy in whole:
            copy.start()

        @pl.when(low)
        def _(chosen=first_half):
            for copy in chosen:
                copy.start()

        @pl.when(jnp.logical_not(low))
        def _(chosen=second_half):
            for copy in chosen:
                copy.start()

        copies = copies + whole + first_half

    if first:
        acc[...] = jnp.zeros_like(acc)
    else:
        acc[pl.ds(0, 64 * TILE)] = c_in[...]

    count = jnp.int32(0)
    for s, delta in enumerate(deltas):
        zs = (z + delta) & (NZ - 1)
        ra = slot(gid(zs, c, 1 - l, h) ^ me)

        def panel(k, count, s=s, zs=zs, ra=ra):
            at = k >> 1
            b_l = l ^ ((at ^ (at >> 1)) & 1)
            b_c = c ^ (k & 1)
            b = b_l * 2 + b_c
            rb = slot(gid(z, h ^ (at >> 1), b_l, b_c) ^ me)
            half = (h ^ (at >> 1) ^ c) * 32
            base = 32 + (zs * 2 + c) * 4
            live_a = meta[ra, b * 8 + 6]
            live_b = meta[rb, base + 2]
            ta = s * tiles + b * SA
            tb = s * 16 + k * 2
            for q in range(SB):
                place = meta[rb, base + q]
                for t in range(SA):
                    index = meta[ra, b * 8 + t]
                    i = index >> 3
                    chunk = ((i >> 2) - y) & 3
                    spot = chunk ^ (chunk >> 1)
                    block = half + (spot * 4 + (i & 3)) * 2 + (place & 1)
                    hit = ((index & 7) == (place >> 1)) & (t < live_a) & (q < live_b)
                    work[count] = (block << 20) | ((tb + q) << 10) | (ta + t)
                    count = count + hit.astype(jnp.int32)
            return count

        count = lax.fori_loop(0, 8, panel, count)
    for k in range(7):
        work[count + k] = jnp.int32(64 << 20)

    for copy in copies:
        copy.wait()

    def rows_of(k):
        return pl.ds(pl.multiple_of(k * TILE, TILE), TILE)

    def products(g, carry):
        for k in range(8):
            w = work[g * 8 + k]
            block = rows_of(w >> 20)
            acc[block] = acc[block] + jnp.dot(
                abuf[rows_of(w & 1023)], bbuf[rows_of((w >> 10) & 1023)], preferred_element_type=jnp.float32
            )
        return carry

    lax.fori_loop(0, (count + 7) >> 3, products, 0)

    for (start, size), out in zip(outs_rows, outs):
        out[...] = acc[pl.ds(start * TILE, size * TILE)]


def multiply(deltas, parts, tiles, ids, meta, lefts, rights, total, outs_rows):
    n = len(deltas)
    first = total is None
    operands = [ids, meta, *lefts, *rights] + ([] if first else [total])
    return pl.pallas_call(
        functools.partial(kernel, deltas, parts, tiles, first, outs_rows),
        out_shape=[jax.ShapeDtypeStruct((k * TILE, TILE), jnp.float32) for _, k in outs_rows],
        in_specs=[SMEM, SMEM] + [HBM] * (len(lefts) + 5) + ([] if first else [VMEM]),
        out_specs=[VMEM] * len(outs_rows),
        scratch_shapes=[
            pltpu.VMEM((n * tiles * TILE, TILE), jnp.bfloat16),
            pltpu.VMEM((n * 16 * TILE, TILE), jnp.bfloat16),
            pltpu.VMEM((65 * TILE, TILE), jnp.float32),
            pltpu.SMEM((n * 96 + 8,), jnp.int32),
            pltpu.SemaphoreType.DMA((len(lefts) + 8 * n,)),
        ],
        compiler_params=pltpu.CompilerParams(vmem_limit_bytes=(24 + 2 * n) * 1024 * 1024),
        cost_estimate=pl.CostEstimate(
            flops=n * 40_000_000, bytes_accessed=8_000_000 + n * 4_000_000, transcendentals=0
        ),
        name="products_%s" % "_".join(str(d & 7) for d in deltas),
    )(*operands)


send = lax.ppermute
barrier = lax.optimization_barrier


def onward(f, b):
    return send(f, "row", z_route(1)), send(b, "row", z_route(-1))


def inner(x):
    return send(x, "col", INNER_ROUTE)


def outer(x):
    return send(x, BOTH, outer_route())


REST = 2 * RIGHT_ROWS - QUARTER


def spread_two(meta, low):
    around = [send(meta, BOTH, [(i, i ^ (k << low)) for i in range(64)]) for k in (1, 2, 3)]
    return jnp.concatenate([meta, *around], axis=0)


def spread(meta, bit):
    return jnp.concatenate([meta, send(meta, BOTH, [(i, i ^ (1 << bit)) for i in range(64)])], axis=0)


def shards(a_tiles, a_index, a_count, b_tiles, b_place, b_count):
    row = lax.axis_index("row")
    col = lax.axis_index("col")
    y = lax.axis_index("depth")
    core = col & 1
    ids = jnp.stack([row >> 1, row & 1, col >> 1, core, y, y, y, y]).astype(jnp.int32)

    own = send(a_tiles.reshape(LEFT_ROWS, TILE), BOTH, swap_route())
    tiles = b_tiles.reshape(NZ, 2, SB * TILE, TILE)
    mine = lax.dynamic_index_in_dim(tiles, core, 1, keepdims=False).reshape(RIGHT_ROWS, TILE)
    theirs = lax.dynamic_index_in_dim(tiles, 1 - core, 1, keepdims=False).reshape(RIGHT_ROWS, TILE)
    right = jnp.concatenate([mine, send(theirs, "col", CORE_ROUTE)], axis=0)
    left_meta = jnp.pad(a_index.reshape(PANELS, SA), ((0, 0), (0, 2))) + jnp.pad(
        a_count.reshape(PANELS, 1), ((0, 0), (6, 1))
    )
    right_meta = jnp.pad(b_place.reshape(16, SB), ((0, 0), (0, 2))) + jnp.pad(
        b_count.reshape(16, 1), ((0, 0), (2, 1))
    )
    meta = jnp.concatenate(
        [left_meta.reshape(1, 32), right_meta.reshape(1, 64), jnp.zeros((1, 32), jnp.int32)], axis=1
    )
    meta = spread_two(spread_two(meta, 3), 1)
    own, right, meta = barrier((own, right, meta))

    f1, b1 = onward(own, own)
    in1, out1 = inner(right[QUARTER:]), outer(right[:REST])
    meta = spread(spread(meta, BITS[4]), BITS[5])
    f1, b1, meta = barrier((f1, b1, meta))

    f2, b2 = onward(f1, b1)
    in2 = jnp.concatenate([right[:QUARTER], out1[:RIGHT_ROWS]], axis=0)
    out2 = jnp.concatenate([right[REST:], in1[RIGHT_ROWS - QUARTER :]], axis=0)
    in2, out2 = inner(in2), outer(out2)
    f2, b2 = barrier((f2, b2))

    f3, b3 = onward(f2, b2)
    rights = [right, in1, in2, out1, out2]
    one = ((0, LEFT_ROWS),)
    whole = ((0, 64),)
    (total,) = multiply((0, -1, 1), one, ATILES, ids, meta, [own, f1, b1], rights, None, whole)
    f3, b3, total = barrier((f3, b3, total))
    far = [send(jnp.where(core == 0, f3, b3), BOTH, far_route())]
    (total,) = multiply((-2, 2, -3, 3), one, ATILES, ids, meta, [f2, b2, f3, b3], rights, total, whole)
    kept, other = multiply((4,), one, ATILES, ids, meta, far, rights, total, ((0, 32), (32, 32)))

    other = send(other, "col", CORE_ROUTE)
    half = 4 * TILE

    def unit(k, count=1):
        rows = slice(k * half, (k + count) * half)
        return kept[rows] + other[rows]

    units = barrier((unit(6), unit(7), unit(3), unit(4)))
    up2 = send(units[0], "depth", y_route(1))
    down2 = send(units[1], "depth", y_route(-1))
    up1 = send(units[2], ALL, home_route(1))
    down1 = send(units[3], ALL, home_route(-1))
    still = send(unit(0, 2), BOTH, swap_route())
    up2, down2 = barrier((up2, down2))
    up3 = send(unit(2) + up2, ALL, home_route(1))
    down3 = send(unit(5) + down2, ALL, home_route(-1))
    low = still[:half] + down1 + up3
    high = still[half:] + up1 + down3
    return jnp.concatenate([low, high], axis=0).reshape(4, 2, TILE, TILE)


def solution(mesh):
    placed = (
        P("row", "col", "depth", None, None, None, None),
        P("row", "col", "depth", None, None),
        P("row", "col", "depth", None),
        P("row", "col", "depth", None, None, None, None),
        P("row", "col", "depth", None, None),
        P("row", "col", "depth", None),
    )
    return jax.shard_map(
        shards,
        mesh=mesh,
        in_specs=placed,
        out_specs=P(("col", "depth"), "row", None, None),
        check_vma=False,
    )
```
